32 devices in a mesh: dp: 8 (over z, x), ctx: 2 (over core), tp: 2 (over y).
Axes of the slice: x: 2, y: 2, z: 4, core: 2. Of those that a mesh axis runs over, the one named last changes fastest.
Arguments:
- hidden_in: bfloat16 [16, 1024, 1024], P('dp', 'ctx'), may hold values from -6 to 6
- cotangent: bfloat16 [16, 1024, 1024], P('dp', 'ctx'), may hold values from -6 to 6
- attn_norm_gain: float32 [1024], replicated, may hold values from 0.5 to 1.5
- ffn_norm_gain: float32 [1024], replicated, may hold values from 0.5 to 1.5
- w_query: bfloat16 [1024, 512], P(('dp', 'ctx'), 'tp'), may hold values from -0.1875 to 0.1875
- key_weight: bfloat16 [1024, 128], P(('dp', 'ctx'), 'tp'), may hold values from -0.1875 to 0.1875
- value_weight: bfloat16 [1024, 128], P(('dp', 'ctx'), 'tp'), may hold values from -0.1875 to 0.1875
- w_attn_out: bfloat16 [512, 1024], P('tp', ('dp', 'ctx')), may hold values from -2 to 2
- mixer_input_weight: bfloat16 [1024, 1536], P(('dp', 'ctx'), 'tp'), may hold values from -0.1875 to 0.1875
- mixer_gate_weight: bfloat16 [1024, 1536], P(('dp', 'ctx'), 'tp'), may hold values from -0.1875 to 0.1875
- w_ssm_bc: bfloat16 [1024, 256], P(('dp', 'ctx')), may hold values from -0.1875 to 0.1875
- w_ssm_dt: bfloat16 [1024, 24], P(('dp', 'ctx'), 'tp'), may hold values from -0.1875 to 0.1875
- dt_bias: float32 [24], P('tp'), may hold values from -4 to -1
- a_log: float32 [24], P('tp'), may hold values from -2 to 1.5
- d_skip: float32 [24], P('tp'), may hold values from 0.5 to 1.5
- input_conv_taps: float32 [4, 1536], P(None, 'tp'), may hold values from -3 to 3
- conv_bc: float32 [4, 256], replicated, may hold values from -3 to 3
- mixer_output_weight: bfloat16 [1536, 1024], P('tp', ('dp', 'ctx')), may hold values from -0.4375 to 0.4375
- w_gate: bfloat16 [1024, 2048], P(('dp', 'ctx'), 'tp'), may hold values from -0.1875 to 0.1875
- w_up: bfloat16 [1024, 2048], P(('dp', 'ctx'), 'tp'), may hold values from -0.1875 to 0.1875
- w_down: bfloat16 [2048, 1024], P('tp', ('dp', 'ctx')), may hold values from -0.25 to 0.25
Outputs:
- out: bfloat16 [16, 1024, 1024], P('dp', 'ctx')
- grad_in: bfloat16 [16, 1024, 1024], P('dp', 'ctx')
- grad_attn_norm_gain: float32 [1024], replicated
- grad_ffn_norm_gain: float32 [1024], replicated
- grad_w_query: float32 [1024, 512], P(('dp', 'ctx'), 'tp')
- grad_w_key: float32 [1024, 128], P(('dp', 'ctx'), 'tp')
- grad_w_value: float32 [1024, 128], P(('dp', 'ctx'), 'tp')
- grad_w_attn_out: float32 [512, 1024], P('tp', ('dp', 'ctx'))
- grad_w_ssm_x: float32 [1024, 1536], P(('dp', 'ctx'), 'tp')
- grad_w_ssm_gate: float32 [1024, 1536], P(('dp', 'ctx'), 'tp')
- grad_w_ssm_bc: float32 [1024, 256], P(('dp', 'ctx'))
- grad_w_ssm_dt: float32 [1024, 24], P(('dp', 'ctx'), 'tp')
- grad_dt_bias: float32 [24], P('tp')
- grad_a_log: float32 [24], P('tp')
- grad_d_skip: float32 [24], P('tp')
- grad_conv_x: float32 [4, 1536], P(None, 'tp')
- grad_conv_bc: float32 [4, 256], replicated
- grad_w_ssm_out: float32 [1536, 1024], P('tp', ('dp', 'ctx'))
- grad_w_gate: float32 [1024, 2048], P(('dp', 'ctx'), 'tp')
- grad_w_up: float32 [1024, 2048], P(('dp', 'ctx'), 'tp')
- grad_w_down: float32 [2048, 1024], P('tp', ('dp', 'ctx'))
The draws below stay inside these ranges and needn't reach their ends.
All inputs are finite; a program needn't handle non-finite values.
Results may differ from the reference program's by a relative error of at most 0.018.
Values may be sent and summed in bfloat16 or wider, within the bound.
A program may use at most 192 MiB of HBM per device.

```python
import jax
import jax.numpy as jnp
from jax import lax

MODEL_WIDTH = 1024
QUERY_HEADS = 8
KEY_VALUE_HEADS = 2
ATTN_HEAD_SIZE = 64
MIXER_HEADS = 24
MIXER_HEAD_SIZE = 64
NS = 128
FF = 2048
CONV_TAPS = 4
SPAN = 256
SEQUENCE_LENGTH = 1024
SEQS = 16


def steps_of(stream_key, shape, split, least, high):
    def one(dim, parts):
        draws = jax.random.uniform(jax.random.fold_in(jax.random.fold_in(stream_key, 6), dim), (parts,), jnp.float32, least / len(split), high / len(split))
        return jnp.repeat(jnp.exp(draws), shape[dim] // parts).reshape((-1,) + (1,) * (len(shape) - dim - 1))

    factor_of = one(*split[0])
    for cut in split[1:]:
        factor_of = factor_of * one(*cut)
    return factor_of


def scatter_about(own_key, extent, width, limit, split=(), kind=jnp.bfloat16):
    values = jax.random.normal(own_key, extent, jnp.float32) * width
    if len(split) > 0:
        values = steps_of(own_key, extent, split, -0.22, 0.18) * values
    return jnp.clip(values, min=-limit, max=limit).astype(kind)


def setup_inputs(seed: int = 0) -> dict:
    splits = jax.random.split(jax.random.key(seed), 22)
    return {
        "hidden_in": scatter_about(splits[0], (SEQS, SEQUENCE_LENGTH, MODEL_WIDTH), 1.0, 6.0, ((0, 8), (1, 2))),
        "cotangent": scatter_about(splits[1], (SEQS, SEQUENCE_LENGTH, MODEL_WIDTH), 1.0, 6.0, ((0, 8), (1, 2))),
        "attn_norm_gain": jnp.clip(1.0 + 0.1 * jax.random.normal(splits[2], (MODEL_WIDTH,), jnp.float32), 0.5, 1.5),
        "ffn_norm_gain": jnp.clip(1.0 + 0.1 * jax.random.normal(splits[3], (MODEL_WIDTH,), jnp.float32), 0.5, 1.5),
        "w_query": scatter_about(splits[4], (MODEL_WIDTH, QUERY_HEADS * ATTN_HEAD_SIZE), MODEL_WIDTH ** -0.5, 0.1875, ((0, 16), (1, 2))),
        "key_weight": scatter_about(splits[5], (MODEL_WIDTH, KEY_VALUE_HEADS * ATTN_HEAD_SIZE), MODEL_WIDTH ** -0.5, 0.1875, ((0, 16), (1, 2))),
        "value_weight": scatter_about(splits[6], (MODEL_WIDTH, KEY_VALUE_HEADS * ATTN_HEAD_SIZE), MODEL_WIDTH ** -0.5, 0.1875, ((0, 16), (1, 2))),
        "w_attn_out": scatter_about(splits[7], (QUERY_HEADS * ATTN_HEAD_SIZE, MODEL_WIDTH), (max(1, QUERY_HEADS * ATTN_HEAD_SIZE // 64)) ** -0.5, 2.0, ((0, 2), (1, 16))),
        "mixer_input_weight": scatter_about(splits[8], (MODEL_WIDTH, MIXER_HEADS * MIXER_HEAD_SIZE), MODEL_WIDTH ** -0.5, 0.1875, ((0, 16), (1, 2))),
        "mixer_gate_weight": scatter_about(splits[9], (MODEL_WIDTH, MIXER_HEADS * MIXER_HEAD_SIZE), MODEL_WIDTH ** -0.5, 0.1875, ((0, 16), (1, 2))),
        "w_ssm_bc": scatter_about(splits[10], (MODEL_WIDTH, 2 * NS), MODEL_WIDTH ** -0.5, 0.1875, ((0, 16),)),
        "w_ssm_dt": scatter_about(splits[11], (MODEL_WIDTH, MIXER_HEADS), MODEL_WIDTH ** -0.5, 0.1875, ((0, 16), (1, 2))),
        "dt_bias": jnp.clip(-4.0 + 3.0 * jax.random.uniform(splits[12], (MIXER_HEADS,), jnp.float32) ** steps_of(splits[12], (MIXER_HEADS,), ((0, 2),), -0.2, 0.2), -4.0, -1.0),
        "a_log": jnp.clip(-2.0 + 3.5 * jax.random.uniform(splits[13], (MIXER_HEADS,), jnp.float32) ** steps_of(splits[13], (MIXER_HEADS,), ((0, 2),), -0.2, 0.2), -2.0, 1.5),
        "d_skip": jnp.clip(0.5 + 1.0 * jax.random.uniform(splits[14], (MIXER_HEADS,), jnp.float32) ** steps_of(splits[14], (MIXER_HEADS,), ((0, 2),), -0.2, 0.2), 0.5, 1.5),
        "input_conv_taps": scatter_about(splits[15], (CONV_TAPS, MIXER_HEADS * MIXER_HEAD_SIZE), CONV_TAPS ** -0.5, 3.0, ((1, 2),), jnp.float32),
        "conv_bc": scatter_about(splits[16], (CONV_TAPS, 2 * NS), CONV_TAPS ** -0.5, 3.0, (), jnp.float32),
        "mixer_output_weight": scatter_about(splits[17], (MIXER_HEADS * MIXER_HEAD_SIZE, MODEL_WIDTH), (MIXER_HEADS * MIXER_HEAD_SIZE // 8) ** -0.5, 0.4375, ((0, 2), (1, 16))),
        "w_gate": scatter_about(splits[18], (MODEL_WIDTH, FF), MODEL_WIDTH ** -0.5, 0.1875, ((0, 16), (1, 2))),
        "w_up": scatter_about(splits[19], (MODEL_WIDTH, FF), MODEL_WIDTH ** -0.5, 0.1875, ((0, 16), (1, 2))),
        "w_down": scatter_about(splits[20], (FF, MODEL_WIDTH), (FF // 4) ** -0.5, 0.25, ((0, 2), (1, 16))),
    }


TOP_PRECISION = lax.Precision.HIGHEST
EPSILON = 1e-05
ROPE_BASE = 10000.0

@jax.custom_vjp
def low(v):
    return lax.optimization_barrier(v.astype(jnp.bfloat16)).astype(jnp.float32)

@jax.custom_vjp
def lower_backward(v):
    return v

def low_keep(v):
    return (low(v), None)

def low_pass(kept, grad):
    return (grad,)

def back_keep(v):
    return (v, None)

def back_low(kept, grad):
    return (low(grad),)
low.defvjp(low_keep, low_pass)
lower_backward.defvjp(back_keep, back_low)

def rms_scale(values, gain_row):
    return values * lax.rsqrt(lax.optimization_barrier(jnp.mean(values * values, axis=-1, keepdims=True)) + EPSILON) * gain_row

def rope_turn(values):
    half_dim = values.shape[-1] // 2
    position = jnp.arange(values.shape[0], dtype=jnp.float32)
    frequency = ROPE_BASE ** (-jnp.arange(half_dim, dtype=jnp.float32) / half_dim)
    angles = position[:, None] * frequency[None, :]
    cosine = jnp.cos(angles)[:, None, :]
    sine_part = jnp.sin(angles)[:, None, :]
    first_half = values[..., :half_dim]
    second_half = values[..., half_dim:]
    return jnp.concatenate([first_half * cosine - second_half * sine_part, second_half * cosine + first_half * sine_part], axis=-1)

def attend_one(queries, key_rows, value_rows):
    length = queries.shape[0]
    turned_queries = lower_backward(low(rope_turn(queries)))
    turned_keys = lower_backward(low(rope_turn(key_rows)))
    scores = jnp.einsum('qhd,khd->hqk', turned_queries, turned_keys, precision=TOP_PRECISION) * queries.shape[-1] ** (-0.5)
    positions = jnp.arange(length)
    causal = positions[None, :] <= positions[:, None]
    scores = jnp.where(causal[None, :, :], scores, -1e+30)
    weights = lower_backward(low(jax.nn.softmax(scores, axis=-1)))
    return jnp.einsum('hqk,khd->qhd', weights, value_rows, precision=TOP_PRECISION)

def block_step(carry_state, pieces):
    ssm_heads, write_rows, read_rows, step_size, log_decay = pieces
    cumulative = jnp.cumsum(log_decay, axis=0)
    block_rows = cumulative.shape[0]
    log_gap = cumulative[:, None, :] - cumulative[None, :, :]
    positions = jnp.arange(block_rows)
    lower_mask = (positions[None, :] <= positions[:, None])[:, :, None]
    decay_table = jnp.exp(jnp.where(lower_mask, log_gap, -1e+30))
    pairing = jnp.einsum('tn,sn->ts', read_rows, write_rows, precision=TOP_PRECISION)
    mixing = pairing[:, :, None] * decay_table * step_size[None, :, :]
    within = jnp.einsum('tsh,shp->thp', mixing, ssm_heads, precision=TOP_PRECISION)
    carried = jnp.einsum('tn,hpn->thp', read_rows, carry_state, precision=TOP_PRECISION) * jnp.exp(cumulative)[:, :, None]
    last_row = cumulative[block_rows - 1]
    tail_weight = jnp.exp(last_row[None, :] - cumulative) * step_size
    new_state = jnp.exp(last_row)[:, None, None] * carry_state + jnp.einsum('sh,shp,sn->hpn', tail_weight, ssm_heads, write_rows, precision=TOP_PRECISION)
    return (new_state, within + carried)

def ssd_one(mixer_input, shared_in, dt_raw, dt_shift, log_rate, skip_gain, conv_ssm, conv_common):
    length = mixer_input.shape[0]
    head_count = dt_raw.shape[-1]
    head_dim = mixer_input.shape[-1] // head_count
    state_dim = shared_in.shape[-1] // 2
    joined = jnp.concatenate([mixer_input, shared_in], axis=-1)
    kernel = jnp.concatenate([conv_ssm, conv_common], axis=-1)
    tap_count = kernel.shape[0]
    padded = jnp.pad(joined, ((tap_count - 1, 0), (0, 0)))
    convolved = kernel[0] * padded[0:length]
    for offset in range(1, tap_count):
        convolved = convolved + kernel[offset] * padded[offset:offset + length]
    active = jax.nn.silu(convolved)
    split_at = head_count * head_dim
    ssm_heads = active[:, :split_at].reshape(length, head_count, head_dim)
    write_rows = active[:, split_at:split_at + state_dim]
    read_rows = active[:, split_at + state_dim:]
    step_size = jax.nn.softplus(dt_raw + dt_shift)
    log_decay = -step_size * jnp.exp(log_rate)
    blocks = length // SPAN
    pieces = (ssm_heads.reshape(blocks, SPAN, head_count, head_dim), write_rows.reshape(blocks, SPAN, state_dim), read_rows.reshape(blocks, SPAN, state_dim), step_size.reshape(blocks, SPAN, head_count), log_decay.reshape(blocks, SPAN, head_count))
    start_state = jnp.zeros((head_count, head_dim, state_dim), jnp.float32)
    final_state, outputs = lax.scan(jax.checkpoint(block_step), start_state, pieces)
    result = outputs.reshape(length, head_count, head_dim) + skip_gain[None, :, None] * ssm_heads
    return result.reshape(length, head_count * head_dim)

def project(incoming_rows, weight_matrix):
    return jnp.einsum('ibr,ro->ibo', incoming_rows, weight_matrix, precision=TOP_PRECISION)

def layer(hidden, params):
    attn_gain, ffn_gain, w_query, key_weight, value_weight, w_attn_out, mixer_input_weight, mixer_gate_weight, w_ssm_bc, w_ssm_dt, dt_bias, a_log, d_skip, input_conv_taps, conv_bc, mixer_output_weight, w_gate, w_up, w_down = params
    sharing_count = QUERY_HEADS // KEY_VALUE_HEADS
    normed = low(rms_scale(hidden, attn_gain))
    queries = lower_backward(low(project(normed, w_query)))
    key_rows = lower_backward(low(project(normed, key_weight)))
    value_rows = lower_backward(low(project(normed, value_weight)))
    gate_ssm = lower_backward(project(normed, mixer_gate_weight))
    mixer_input = lower_backward(low(project(normed, mixer_input_weight)))
    shared_rows = lower_backward(low(project(normed, w_ssm_bc)))
    dt_raw = lower_backward(low(project(normed, w_ssm_dt)))

    def attend_seq(pieces):
        query_one, single_key, single_value = pieces
        broadened_keys = jnp.repeat(single_key.reshape(SEQUENCE_LENGTH, KEY_VALUE_HEADS, ATTN_HEAD_SIZE), sharing_count, axis=1)
        broadened_values = lower_backward(jnp.repeat(single_value.reshape(SEQUENCE_LENGTH, KEY_VALUE_HEADS, ATTN_HEAD_SIZE), sharing_count, axis=1))
        return attend_one(query_one.reshape(SEQUENCE_LENGTH, QUERY_HEADS, ATTN_HEAD_SIZE), broadened_keys, broadened_values).reshape(SEQUENCE_LENGTH, QUERY_HEADS * ATTN_HEAD_SIZE)

    def ssd_seq(pieces):
        ssm_one, shared_one, dt_one = pieces
        return ssd_one(ssm_one, shared_one, dt_one, dt_bias, a_log, d_skip, input_conv_taps, conv_bc)
    attended = lower_backward(low(lax.map(jax.checkpoint(attend_seq), (queries, key_rows, value_rows))))
    scan_result = lower_backward(low(lax.map(jax.checkpoint(ssd_seq), (mixer_input, shared_rows, dt_raw))))
    gated_rows = low(scan_result * jax.nn.silu(gate_ssm))
    mixed_sum = lower_backward(project(attended, w_attn_out) + project(gated_rows, mixer_output_weight))
    middle = hidden + mixed_sum
    normed_ffn = low(rms_scale(middle, ffn_gain))
    gate_rows = lower_backward(project(normed_ffn, w_gate))
    up_rows = lower_backward(project(normed_ffn, w_up))
    inner_rows = low(jax.nn.silu(gate_rows) * up_rows)
    return middle + project(inner_rows, w_down)

def reference(hidden_in, cotangent, attn_norm_gain, ffn_norm_gain, w_query, key_weight, value_weight, w_attn_out, mixer_input_weight, mixer_gate_weight, w_ssm_bc, w_ssm_dt, dt_bias, a_log, d_skip, input_conv_taps, conv_bc, mixer_output_weight, w_gate, w_up, w_down):
    params = tuple((weight_matrix.astype(jnp.float32) for weight_matrix in (attn_norm_gain, ffn_norm_gain, w_query, key_weight, value_weight, w_attn_out, mixer_input_weight, mixer_gate_weight, w_ssm_bc, w_ssm_dt, dt_bias, a_log, d_skip, input_conv_taps, conv_bc, mixer_output_weight, w_gate, w_up, w_down)))
    bundle = max((count for count in range(1, SEQS + 1) if SEQS % count == 0 and count * SEQUENCE_LENGTH <= 4096))
    inputs_all = hidden_in.astype(jnp.float32).reshape(SEQS // bundle, bundle, SEQUENCE_LENGTH, MODEL_WIDTH)
    grads_all = cotangent.astype(jnp.float32).reshape(SEQS // bundle, bundle, SEQUENCE_LENGTH, MODEL_WIDTH)

    def group_step(totals, batch_in):
        hidden_part, grad_part = batch_in
        result, pullback = jax.vjp(layer, hidden_part, params)
        grad_hidden, grad_params = pullback(grad_part)
        totals = tuple((running + update for running, update in zip(totals, grad_params)))
        return (totals, (result.astype(jnp.bfloat16), grad_hidden.astype(jnp.bfloat16)))
    start_totals = tuple((jnp.zeros_like(weight_matrix) for weight_matrix in params))
    totals, (results, grad_hiddens) = lax.scan(group_step, start_totals, (inputs_all, grads_all))
    return (results.reshape(SEQS, SEQUENCE_LENGTH, MODEL_WIDTH), grad_hiddens.reshape(SEQS, SEQUENCE_LENGTH, MODEL_WIDTH), totals[0], totals[1], totals[2], totals[3], totals[4], totals[5], totals[6], totals[7], totals[8], totals[9], totals[10], totals[11], totals[12], totals[13], totals[14], totals[15], totals[16], totals[17], totals[18])
```

```python
import jax
import jax.numpy as jnp
from jax import lax
from jax.sharding import PartitionSpec as P

QUERY_HEADS = 8
KEY_VALUE_HEADS = 2
ATTN_HEAD_SIZE = 64
MIXER_HEAD_SIZE = 64
NS = 128
CONV_TAPS = 4
SPAN = 256


TOP_PRECISION = lax.Precision.HIGHEST
EPSILON = 1e-05
ROPE_BASE = 10000.0


def rms_scale(values, gain_row):
    return (
        values * lax.rsqrt(jnp.mean(values * values, axis=-1, keepdims=True) + EPSILON) * gain_row
    )


def rope_turn(values):
    half_dim = values.shape[-1] // 2
    position = jnp.arange(values.shape[0], dtype=jnp.float32)
    frequency = ROPE_BASE ** (-jnp.arange(half_dim, dtype=jnp.float32) / half_dim)
    angles = position[:, None] * frequency[None, :]
    cosine = jnp.cos(angles)[:, None, :]
    sine_part = jnp.sin(angles)[:, None, :]
    first_half = values[..., :half_dim]
    second_half = values[..., half_dim:]
    return jnp.concatenate(
        [
            first_half * cosine - second_half * sine_part,
            second_half * cosine + first_half * sine_part,
        ],
        axis=-1,
    )


def attend(queries, key_rows, value_rows):
    batch, length, kv_count, group, head_dim = queries.shape
    turn = jax.vmap(rope_turn)
    turned_queries = turn(
        queries.reshape(batch, length, kv_count * group, head_dim).astype(jnp.float32)
    ).astype(jnp.bfloat16)
    turned_queries = turned_queries.reshape(queries.shape)
    turned_keys = turn(key_rows.astype(jnp.float32)).astype(jnp.bfloat16)
    scores = jnp.einsum(
        "bqcgd,bkcd->bcgqk", turned_queries, turned_keys, preferred_element_type=jnp.float32
    ) * head_dim ** (-0.5)
    positions = jnp.arange(length)
    causal = positions[None, :] <= positions[:, None]
    scores = jnp.where(causal, scores, -1e30)
    weights = jax.nn.softmax(scores, axis=-1).astype(jnp.bfloat16)
    return jnp.einsum(
        "bcgqk,bkcd->bqcgd", weights, value_rows, preferred_element_type=jnp.float32
    )


def bf(values):
    return values.astype(jnp.bfloat16)


def ein(form, *operands):
    return jnp.einsum(form, *operands, preferred_element_type=jnp.float32)


def conv_silu(values, taps):
    length = values.shape[1]
    tap_count = taps.shape[0]
    padded = jnp.pad(values, ((0, 0), (tap_count - 1, 0), (0, 0))).astype(jnp.float32)
    convolved = taps[0] * padded[:, 0:length]
    for offset in range(1, tap_count):
        convolved = convolved + taps[offset] * padded[:, offset : offset + length]
    return jax.nn.silu(convolved)


def ssd(mixer_input, shared_in, dt_raw, dt_shift, log_rate, skip_gain, conv_ssm, conv_common):
    batch, length, head_count = dt_raw.shape
    head_dim = mixer_input.shape[-1] // head_count
    state_dim = shared_in.shape[-1] // 2
    blocks = length // SPAN
    heads_last = conv_silu(mixer_input, conv_ssm).reshape(
        batch, blocks, SPAN, head_count, head_dim
    )
    ssm_heads = heads_last.transpose(0, 1, 3, 2, 4)
    common = conv_silu(shared_in, conv_common).reshape(batch, blocks, SPAN, 2 * state_dim)
    write_rows = bf(common[..., :state_dim])
    read_rows = bf(common[..., state_dim:])
    step_size = jax.nn.softplus(dt_raw.astype(jnp.float32) + dt_shift)
    step_size = step_size.reshape(batch, blocks, SPAN, head_count).transpose(0, 1, 3, 2)
    log_decay = -step_size * jnp.exp(log_rate)[:, None]
    positions = jnp.arange(SPAN)
    lower_mask = positions[None, :] <= positions[:, None]
    cumulative = jnp.einsum(
        "bkhs,ts->bkht", log_decay, lower_mask.astype(jnp.float32), precision=TOP_PRECISION
    )
    log_gap = cumulative[..., :, None] - cumulative[..., None, :]
    decay_table = jnp.exp(jnp.where(lower_mask, log_gap, -1e30))
    pairing = ein("bktn,bksn->bkts", read_rows, write_rows)
    mixing = bf(pairing[:, :, None] * decay_table * step_size[..., None, :])
    heads_low = bf(ssm_heads)
    within = ein("bkhts,bkhsp->bkhtp", mixing, heads_low)
    last = cumulative[..., -1]
    tail_weight = jnp.exp(last[..., None] - cumulative) * step_size
    added = ein("bkhsp,bksn->bkhpn", bf(ssm_heads * tail_weight[..., None]), write_rows)
    states = [jnp.zeros_like(added[:, 0])]
    for block in range(blocks - 1):
        states.append(jnp.exp(last[:, block])[..., None, None] * states[-1] + added[:, block])
    carry_state = jnp.stack(states, axis=1)
    carried = ein("bktn,bkhpn->bkhtp", read_rows, bf(carry_state)) * jnp.exp(cumulative)[..., None]
    result = within + carried + skip_gain[:, None, None] * ssm_heads
    return bf(result).transpose(0, 1, 3, 2, 4).reshape(batch, length, head_count * head_dim)


def plain_dot(operand, weight_matrix):
    return jnp.dot(operand, weight_matrix, preferred_element_type=jnp.float32)


def dot_back(operand, weight_matrix):
    return lax.dot_general(
        operand, weight_matrix, (((1,), (1,)), ((), ())), preferred_element_type=jnp.float32
    )


def dot_left(operand, weight_matrix):
    return lax.dot_general(
        operand, weight_matrix, (((0,), (0,)), ((), ())), preferred_element_type=jnp.float32
    )


def gate_silu(gate_in, other_rows):
    return jax.nn.silu(gate_in) * other_rows


SWAP = [(0, 1), (1, 0)]


def take_sequences(values):
    me = lax.axis_index("ctx")
    count, half, width = values.shape
    share = count // 2
    mine = lax.dynamic_slice_in_dim(values, me * share, share, 0)
    sent = lax.dynamic_slice_in_dim(values, (1 - me) * share, share, 0)
    got = lax.ppermute(sent, "ctx", SWAP)
    whole = jnp.zeros((share, 2 * half, width), values.dtype)
    whole = lax.dynamic_update_slice_in_dim(whole, mine, me * half, 1)
    return lax.dynamic_update_slice_in_dim(whole, got, (1 - me) * half, 1)


def give_positions(values):
    me = lax.axis_index("ctx")
    share, length, width = values.shape
    half = length // 2
    mine = lax.dynamic_slice_in_dim(values, me * half, half, 1)
    sent = lax.dynamic_slice_in_dim(values, (1 - me) * half, half, 1)
    got = lax.ppermute(sent, "ctx", SWAP)
    whole = jnp.zeros((2 * share, half, width), values.dtype)
    whole = lax.dynamic_update_slice_in_dim(whole, mine, me * share, 0)
    return lax.dynamic_update_slice_in_dim(whole, got, (1 - me) * share, 0)


def tp_sum(values):
    own = lax.optimization_barrier(bf(values))
    other = lax.ppermute(own, "tp", SWAP)
    return own.astype(jnp.float32) + other.astype(jnp.float32)


def gather_rows(shard):
    rows, columns = shard.shape
    over_dp = lax.all_gather(shard, "dp", axis=0, tiled=False)
    both = lax.all_gather(over_dp, "ctx", axis=1, tiled=True)
    return both.reshape(-1, columns)


def split_rows(values, rows):
    me = lax.axis_index("ctx")
    parts = values.reshape(values.shape[0], -1, 2, rows)
    mine = lax.dynamic_index_in_dim(parts, me, 2, False)
    other = lax.dynamic_index_in_dim(parts, 1 - me, 2, False)
    return mine.reshape(values.shape[0], -1), other.reshape(values.shape[0], -1)


def core_sum(left, right, rows):
    mine, other = split_rows(left, rows)
    got = lax.ppermute(bf(dot_left(other, right)), "ctx", SWAP)
    return bf(dot_left(mine, right) + got.astype(jnp.float32))


def dp_scatter(values):
    return lax.psum_scatter(values, "dp", scatter_dimension=0, tiled=True).astype(jnp.float32)


def per_device(
    hidden_in,
    cotangent,
    attn_norm_gain,
    ffn_norm_gain,
    w_query,
    key_weight,
    value_weight,
    w_attn_out,
    mixer_input_weight,
    mixer_gate_weight,
    w_ssm_bc,
    w_ssm_dt,
    dt_bias,
    a_log,
    d_skip,
    input_conv_taps,
    conv_bc,
    mixer_output_weight,
    w_gate,
    w_up,
    w_down,
):
    sequence_count, halved_length, model_width = hidden_in.shape
    tp_index = lax.axis_index("tp")
    batch = sequence_count // 2
    length = halved_length * 2
    count_of_rows = batch * length
    shard_rows = w_query.shape[0]
    q_w = w_query.shape[1]
    kv_w = key_weight.shape[1]
    x_w = mixer_input_weight.shape[1]
    bc_w = w_ssm_bc.shape[1]
    local_mixer = w_ssm_dt.shape[1]
    ff_w = w_gate.shape[1]
    local_kv = kv_w // ATTN_HEAD_SIZE
    group = q_w // kv_w
    dt_w = -(-local_mixer // 128) * 128
    edges = [0]
    for width in (x_w, q_w, bc_w, kv_w, kv_w, dt_w, x_w):
        edges.append(edges[-1] + width)
    gate_at = edges[6]

    in_shard = jnp.concatenate(
        [
            mixer_input_weight,
            w_query,
            w_ssm_bc,
            key_weight,
            value_weight,
            jnp.pad(w_ssm_dt, ((0, 0), (0, dt_w - local_mixer))),
            mixer_gate_weight,
        ],
        axis=1,
    )
    rest_shard = jnp.concatenate(
        [w_attn_out.T, mixer_output_weight.T, w_gate, w_up, w_down.T], axis=1
    )
    full_in = gather_rows(in_shard)
    full_rest = gather_rows(rest_shard)
    out_w = q_w + x_w
    full_out = full_rest[:, :out_w]
    full_gate_up = full_rest[:, out_w : out_w + 2 * ff_w]
    full_down = full_rest[:, out_w + 2 * ff_w :]

    hidden = take_sequences(hidden_in).astype(jnp.float32).reshape(count_of_rows, model_width)
    grad_rows = take_sequences(cotangent).reshape(count_of_rows, model_width)

    normed_full, attn_norm_pull = jax.vjp(rms_scale, hidden, attn_norm_gain)
    normed = bf(normed_full)
    projected = bf(plain_dot(normed, full_in[:, :gate_at]))
    gate_ssm = plain_dot(normed, full_in[:, gate_at:])
    pieces = [projected[:, low:high] for low, high in zip(edges[:6], edges[1:7])]
    mixer_input, queries, shared_rows, key_rows, value_rows, dt_raw = pieces
    dt_raw = dt_raw[:, :local_mixer]

    attended, attend_pull = jax.vjp(
        attend,
        queries.reshape(batch, length, local_kv, group, ATTN_HEAD_SIZE),
        key_rows.reshape(batch, length, local_kv, ATTN_HEAD_SIZE),
        value_rows.reshape(batch, length, local_kv, ATTN_HEAD_SIZE),
    )
    scan_result, ssd_pull = jax.vjp(
        ssd,
        mixer_input.reshape(batch, length, x_w),
        shared_rows.reshape(batch, length, bc_w),
        dt_raw.reshape(batch, length, local_mixer),
        dt_bias,
        a_log,
        d_skip,
        input_conv_taps,
        conv_bc,
    )
    attn_rows = bf(attended).reshape(count_of_rows, q_w)
    mixer_rows = scan_result.reshape(count_of_rows, x_w)
    gated_full, gate_pull = jax.vjp(gate_silu, gate_ssm, mixer_rows.astype(jnp.float32))
    mixed_in = jnp.concatenate([attn_rows, bf(gated_full)], axis=1)
    middle = hidden + tp_sum(dot_back(mixed_in, full_out))
    normed_ffn_full, ffn_norm_pull = jax.vjp(rms_scale, middle, ffn_norm_gain)
    normed_ffn = bf(normed_ffn_full)
    gate_up = plain_dot(normed_ffn, full_gate_up)
    inner_full, inner_pull = jax.vjp(gate_silu, gate_up[:, :ff_w], gate_up[:, ff_w:])
    inner_rows = bf(inner_full)

    grad_inner = plain_dot(grad_rows, full_down)
    grad_gate_full, grad_up_full = inner_pull(grad_inner)
    grad_gate_up = jnp.concatenate([bf(grad_gate_full), bf(grad_up_full)], axis=1)
    grad_ffn_partial = dot_back(grad_gate_up, full_gate_up)
    ffn_gain_part = ffn_norm_pull(grad_ffn_partial)[1]
    grad_middle = grad_rows.astype(jnp.float32) + ffn_norm_pull(tp_sum(grad_ffn_partial))[0]
    ffn_sent = jnp.concatenate(
        [
            core_sum(normed_ffn, grad_gate_up, shard_rows),
            core_sum(grad_rows, inner_rows, shard_rows),
        ],
        axis=1,
    )
    ffn_grads = dp_scatter(ffn_sent)

    grad_mixed = bf(grad_middle)
    out_grads = dp_scatter(core_sum(grad_mixed, mixed_in, shard_rows))
    grad_mixed_in = plain_dot(grad_mixed, full_out)
    grad_attn_rows = grad_mixed_in[:, :q_w]
    grad_gate_ssm, mixer_row_gradient = gate_pull(grad_mixed_in[:, q_w:])

    out_partial = dot_back(inner_rows, full_down)
    output = give_positions(
        bf(middle + tp_sum(out_partial)).reshape(batch, length, model_width)
    )

    grad_queries, grad_keys, grad_values = attend_pull(
        bf(grad_attn_rows)
        .astype(jnp.float32)
        .reshape(batch, length, local_kv, group, ATTN_HEAD_SIZE)
    )
    (
        grad_x,
        grad_shared,
        grad_dt,
        grad_shift,
        grad_rate,
        grad_skip,
        grad_conv_x,
        grad_conv_common,
    ) = ssd_pull(bf(mixer_row_gradient).reshape(batch, length, x_w))
    grad_all = jnp.concatenate(
        [
            grad_x.reshape(count_of_rows, x_w),
            grad_queries.reshape(count_of_rows, q_w),
            grad_shared.reshape(count_of_rows, bc_w),
            grad_keys.reshape(count_of_rows, kv_w),
            grad_values.reshape(count_of_rows, kv_w),
            jnp.pad(
                grad_dt.reshape(count_of_rows, local_mixer), ((0, 0), (0, dt_w - local_mixer))
            ),
            bf(grad_gate_ssm),
        ],
        axis=1,
    )
    in_grads = dp_scatter(core_sum(normed, grad_all, shard_rows))
    partial_in = dot_back(grad_all, full_in)
    attn_gain_part = attn_norm_pull(partial_in)[1]
    grad_hidden_norm = attn_norm_pull(tp_sum(partial_in))[0]
    grad_input = give_positions(
        bf(grad_middle + grad_hidden_norm).reshape(batch, length, model_width)
    )

    own = jnp.concatenate([grad_shift, grad_rate, grad_skip, grad_conv_x.reshape(-1)])
    placed = lax.dynamic_update_slice(
        jnp.zeros((lax.axis_size("tp") * own.shape[0],), jnp.float32),
        own,
        (tp_index * own.shape[0],),
    )
    small = jnp.concatenate(
        [attn_gain_part, ffn_gain_part, grad_conv_common.reshape(-1), placed]
    )
    small_size = small.shape[0]
    small = jnp.pad(small, (0, -small_size % 1024)).reshape(-1, 128)
    small = lax.psum(small, ("dp", "ctx", "tp")).reshape(-1)
    conv_size = conv_bc.size
    tail_at = 2 * model_width + conv_size
    own = lax.dynamic_slice(small, (tail_at + tp_index * own.shape[0],), (own.shape[0],))
    in_parts = [in_grads[:, low:high] for low, high in zip(edges[:7], edges[1:8])]
    shared_grad = in_parts[2] + lax.ppermute(in_parts[2], "tp", SWAP)
    return (
        output,
        grad_input,
        small[:model_width],
        small[model_width : 2 * model_width],
        in_parts[1],
        in_parts[3],
        in_parts[4],
        out_grads[:, :q_w].T,
        in_parts[0],
        in_parts[6],
        shared_grad,
        in_parts[5][:, :local_mixer],
        own[:local_mixer],
        own[local_mixer : 2 * local_mixer],
        own[2 * local_mixer : 3 * local_mixer],
        own[3 * local_mixer :].reshape(input_conv_taps.shape),
        small[2 * model_width : tail_at].reshape(conv_bc.shape),
        out_grads[:, q_w:].T,
        ffn_grads[:, :ff_w],
        ffn_grads[:, ff_w : 2 * ff_w],
        ffn_grads[:, 2 * ff_w :].T,
    )


def solution(mesh):
    in_specs = (
        P("dp", "ctx", None),
        P("dp", "ctx", None),
        P(),
        P(),
        P(("dp", "ctx"), "tp"),
        P(("dp", "ctx"), "tp"),
        P(("dp", "ctx"), "tp"),
        P("tp", ("dp", "ctx")),
        P(("dp", "ctx"), "tp"),
        P(("dp", "ctx"), "tp"),
        P(("dp", "ctx"), None),
        P(("dp", "ctx"), "tp"),
        P("tp"),
        P("tp"),
        P("tp"),
        P(None, "tp"),
        P(),
        P("tp", ("dp", "ctx")),
        P(("dp", "ctx"), "tp"),
        P(("dp", "ctx"), "tp"),
        P("tp", ("dp", "ctx")),
    )
    out_specs = (
        P("dp", "ctx", None),
        P("dp", "ctx", None),
        P(),
        P(),
        P(("dp", "ctx"), "tp"),
        P(("dp", "ctx"), "tp"),
        P(("dp", "ctx"), "tp"),
        P("tp", ("dp", "ctx")),
        P(("dp", "ctx"), "tp"),
        P(("dp", "ctx"), "tp"),
        P(("dp", "ctx"), None),
        P(("dp", "ctx"), "tp"),
        P("tp"),
        P("tp"),
        P("tp"),
        P(None, "tp"),
        P(),
        P("tp", ("dp", "ctx")),
        P(("dp", "ctx"), "tp"),
        P(("dp", "ctx"), "tp"),
        P("tp", ("dp", "ctx")),
    )
    return jax.shard_map(
        per_device, mesh=mesh, in_specs=in_specs, out_specs=out_specs, check_vma=False
    )
```
